32 devices in a mesh: depth: 4 (over y, x), shots: 8 (over z, core).
Axes of the slice: x: 2, y: 2, z: 4, core: 2. Of those that a mesh axis runs over, the one named last changes fastest.
Arguments:
- adj_now: float32 [8, 64, 128, 128], P('shots', 'depth'), may hold values from -6 to 6
- adj_prev: float32 [8, 64, 128, 128], P('shots', 'depth'), may hold values from -6 to 6
- fwd_snap: bfloat16 [8, 4, 64, 128, 128], P('shots', None, 'depth'), may hold values from -6 to 6
- velocity: float32 [64, 128, 128], P('depth', 'shots'), may hold values from 1 to 2
- density: float32 [64, 128, 128], P('depth', 'shots'), may hold values from 1 to 2
- shot_count: int32 [8], P('shots'), may hold values from 1 to 12, 32 in all
- rec_x: int32 [8, 256], P('shots'), may hold values from 0 to 127
- rec_y: int32 [8, 256], P('shots'), may hold values from 0 to 127
- residual: float32 [8, 4, 256], P('shots'), may hold values from -6 to 6
Outputs:
- out_now: float32 [8, 64, 128, 128], P('shots', 'depth')
- out_prev: float32 [8, 64, 128, 128], P('shots', 'depth')
- grad_vel: float32 [64, 128, 128], P('depth', 'shots')
The draws below stay inside these ranges and needn't reach their ends.
Inputs may be any that keep to these rules, and one draw needn't show every extreme that they name: `shot_count`: the counts sum to 32; the largest is exactly 12.
All inputs are finite; a program needn't handle non-finite values.
Results may differ from the reference program's by a relative error of at most 0.0003.
Values sent between devices are 32-bit elements; how exact they have to be, the bound alone decides.
A program may use at most 64 MiB of HBM per device.

```python
import math
import jax
import jax.numpy as jnp
import numpy as np
from jax import lax

NX = 128
NY = 128
STEPS = 4
NREC = 256
GROUPS = 8
NZ = 64


def set_ends(array, own_key, smallest, top_value):
    shape = array.shape
    spot = [jax.random.randint(jax.random.fold_in(own_key, axis), (), 0, shape[axis]) for axis in range(len(shape))]
    array = array.at[tuple(spot)].set(smallest)
    longest = shape.index(max(shape))
    spot[longest] = (spot[longest] + 1) % shape[longest]
    return array.at[tuple(spot)].set(top_value)


def shard_levels(stream_key, shape, pieces, low, top_value):
    level = 1.0
    for axis_at, parts in pieces:
        draws = jax.random.uniform(jax.random.fold_in(jax.random.fold_in(stream_key, 6), axis_at), (parts,), jnp.float32, low / len(pieces), top_value / len(pieces))
        level = level * jnp.repeat(jnp.exp(draws), shape[axis_at] // parts).reshape((-1,) + (1,) * (len(shape) - 1 - axis_at))
    return level


def split_up(amount, total, bound, slope):
    portions = [(1 << 20) // math.isqrt(grade ** slope) + 1 for grade in range(2, amount + 1)]
    rest, holding = total - bound - (amount - 1), [1] * (amount - 1)
    while rest > 0:
        movable = [i for i in range(amount - 1) if holding[i] < bound]
        whole, left = sum([portions[i] for i in movable]), rest
        for i in movable:
            more = min(bound - holding[i], max(1, left * portions[i] // whole), rest)
            holding[i] = holding[i] + more
            rest = rest - more
    return np.array([bound] + holding)


def ragged(stream_key, number_of, total, reach, lean):
    if number_of == 2:
        one = jax.random.randint(stream_key, (), max(1, total - reach), min(reach, total - 1) + 1)
        return jnp.stack([one, total - one])
    sizes = jnp.asarray(split_up(number_of, total, reach, lean), jnp.int32)
    pairs = (number_of - 1) // 2
    source_of, taker = sizes[1:1 + 2 * pairs:2], sizes[2:2 + 2 * pairs:2]
    margin = jnp.minimum(source_of - 1, reach - taker)
    moved = jax.random.randint(jax.random.fold_in(stream_key, 1), (pairs,), 0, 1 << 20) % (margin + 1)
    sizes = sizes.at[1:1 + 2 * pairs:2].set(source_of - moved).at[2:2 + 2 * pairs:2].set(taker + moved)
    return sizes[jax.random.permutation(jax.random.fold_in(stream_key, 2), number_of)]


def centred(own_key, extent, deviation, bound, pieces=(), dtype=jnp.bfloat16):
    level = shard_levels(own_key, extent, pieces, -0.22, 0.18) if pieces else 1.0
    entries = jax.random.normal(own_key, extent, jnp.float32) * deviation * level
    return jnp.minimum(jnp.maximum(entries, -bound), bound).astype(dtype)


def setup_inputs(seed: int = 0) -> dict:
    key_list = jax.random.split(jax.random.key(seed), 10)
    return {
        "adj_now": centred(key_list[0], (GROUPS, NZ, NX, NY), 1.0, 6.0, ((0, 8), (1, 4)), jnp.float32),
        "adj_prev": centred(key_list[1], (GROUPS, NZ, NX, NY), 1.0, 6.0, ((0, 8), (1, 4)), jnp.float32),
        "fwd_snap": centred(key_list[2], (GROUPS, STEPS, NZ, NX, NY), 1.0, 6.0, ((0, 8), (2, 4))),
        "velocity": jnp.clip(jnp.exp(math.log(2.0) - 0.6931472 * jax.random.uniform(key_list[3], (NZ, NX, NY), jnp.float32) ** shard_levels(key_list[3], (NZ, NX, NY), ((0, 4), (1, 8)), -0.2, 0.2)), 1.0, 2.0),
        "density": jnp.clip(jnp.exp(math.log(2.0) - 0.6931472 * jax.random.uniform(key_list[4], (NZ, NX, NY), jnp.float32) ** shard_levels(key_list[4], (NZ, NX, NY), ((0, 4), (1, 8)), -0.2, 0.2)), 1.0, 2.0),
        "shot_count": ragged(key_list[5], GROUPS, 4 * GROUPS, 12, 2).astype(jnp.int32),
        "rec_x": set_ends(jax.random.randint(key_list[6], (GROUPS, NREC), 0, NX), jax.random.fold_in(key_list[6], 1), 0, NX - 1).astype(jnp.int32),
        "rec_y": set_ends(jax.random.randint(key_list[7], (GROUPS, NREC), 0, NY), jax.random.fold_in(key_list[7], 1), 0, NY - 1).astype(jnp.int32),
        "residual": centred(key_list[8], (GROUPS, STEPS, NREC), 1.0, 6.0, ((0, 8),), jnp.float32),
    }


def operate(field, buoy):
    padded = jnp.pad(field, 1)
    bpad = jnp.pad(buoy, 1)
    total = jnp.zeros_like(field)
    for axis in range(3):
        center = [slice(1, -1)] * 3
        ahead = list(center)
        behind = list(center)
        ahead[axis] = slice(2, None)
        behind[axis] = slice(0, -2)
        pc, pa, pb = padded[tuple(center)], padded[tuple(ahead)], padded[tuple(behind)]
        bc, ba, bb = bpad[tuple(center)], bpad[tuple(ahead)], bpad[tuple(behind)]
        total = total + 0.5 * (bc + ba) * (pa - pc) - 0.5 * (bb + bc) * (pc - pb)
    return total


def reference(adj_now, adj_prev, fwd_snap, velocity, density, shot_count, rec_x, rec_y, residual):
    kappa = density * velocity * velocity
    buoy = 1.0 / density

    def one_group(items):
        cur, old, snaps, count, rx, ry, res = items
        image = jnp.zeros_like(cur)
        for step in range(STEPS):
            t = STEPS - 1 - step
            plane = jnp.zeros((NX, NY), jnp.float32).at[rx, ry].add(res[t])
            source = jnp.zeros_like(cur).at[2].set(plane)
            new = 2.0 * cur - old + 0.08 * kappa * operate(cur, buoy) + 0.08 * source
            image = image + snaps[t].astype(jnp.float32) * new
            old = cur
            cur = new
        return cur, old, count.astype(jnp.float32) * image

    def scan_body(total, items):
        cur, old, weighted = one_group(items)
        return total + weighted, (cur, old)

    total, (out_now, out_prev) = lax.scan(scan_body, jnp.zeros((NZ, NX, NY), jnp.float32), (adj_now, adj_prev, fwd_snap, shot_count, rec_x, rec_y, residual))
    grad_vel = 2.0 * density * velocity * total / (4.0 * GROUPS)
    return out_now, out_prev, grad_vel
```

```python
import functools
import jax
import jax.numpy as jnp
from jax import lax
from jax.experimental import pallas as pl
from jax.experimental.pallas import tpu as pltpu
from jax.sharding import PartitionSpec as P


def with_halo(shard, sides, width):
    for axis, dim in sides:
        peers, length = (lax.axis_size(axis), shard.shape[dim])
        up = [(i, (i + 1) % peers) for i in range(peers - 1)]
        down = [(j, i) for i, j in up]
        last = lax.slice_in_dim(shard, length - width, length, axis=dim)
        first = lax.slice_in_dim(shard, 0, width, axis=dim)
        before = lax.ppermute(last, axis, up)
        after = lax.ppermute(first, axis, down)
        shard = jnp.concatenate([before, shard, after], axis=dim)
    return shard


def operate(field, buoy):
    padded = jnp.pad(field, 1)
    bpad = jnp.pad(buoy, 1)
    total = jnp.zeros_like(field)
    for axis in range(3):
        center = [slice(1, -1)] * 3
        ahead = list(center)
        behind = list(center)
        ahead[axis] = slice(2, None)
        behind[axis] = slice(0, -2)
        pc, pa, pb = (padded[tuple(center)], padded[tuple(ahead)], padded[tuple(behind)])
        bc, ba, bb = (bpad[tuple(center)], bpad[tuple(ahead)], bpad[tuple(behind)])
        total = total + 0.5 * (bc + ba) * (pa - pc) - 0.5 * (bb + bc) * (pc - pb)
    return total


def source_plane(rows_x, rows_y, amounts, width_x, width_y):
    onehot_x = (rows_x[:, None] == jnp.arange(width_x, dtype=jnp.int32)[None, :]).astype(
        jnp.float32
    )
    onehot_y = (rows_y[:, None] == jnp.arange(width_y, dtype=jnp.int32)[None, :]).astype(
        jnp.float32
    )
    return jnp.dot((onehot_x * amounts[:, None]).T, onehot_y, precision=lax.Precision.HIGHEST)


def body(adj_now, adj_prev, fwd_snap, velocity, density, shot_count, rec_x, rec_y, residual):
    depth_planes = adj_now.shape[1]
    width_x = adj_now.shape[2]
    width_y = adj_now.shape[3]
    steps = fwd_snap.shape[1]
    groups = lax.axis_size("shots")
    width = 1
    vel_all, rho_all = (
        lax.all_gather(velocity, "shots", axis=1, tiled=True),
        lax.all_gather(density, "shots", axis=1, tiled=True),
    )
    packed = jnp.stack([rho_all * vel_all * vel_all, 1.0 / rho_all])
    extended = with_halo(packed, (("depth", 1),), width)
    buoy_ext = extended[1]
    first = lax.axis_index("depth") * depth_planes
    snaps = fwd_snap[0]
    rows_x = rec_x[0]
    rows_y = rec_y[0]
    image = jnp.zeros((depth_planes, width_x, width_y), jnp.float32)
    kappa_ext = extended[0, width : width + depth_planes]
    global_plane = first + jnp.arange(depth_planes, dtype=jnp.int32)
    at_receivers = (global_plane == 2).astype(jnp.float32)[:, None, None]
    current = adj_now[0]
    older = adj_prev[0]
    for step in range(steps):
        moment = steps - 1 - step
        rimmed_field = with_halo(current[None], (("depth", 1),), 1)[0]
        plane = source_plane(rows_x, rows_y, residual[0, moment], width_x, width_y)
        spread = operate(rimmed_field, buoy_ext)[1:-1]
        newer = (
            2.0 * current - older + 0.08 * kappa_ext * spread + 0.08 * at_receivers * plane[None]
        )
        image = image + snaps[moment].astype(jnp.float32) * newer
        older = current
        current = newer
    weighted = shot_count[0].astype(jnp.float32) * image
    summed = lax.psum_scatter(weighted, "shots", scatter_dimension=1, tiled=True)
    grad_vel = 2.0 * density * velocity * summed / (4.0 * groups)
    return (current[None], older[None], grad_vel)


MESH = pl.DeviceIdType.MESH


def kernel(
    depths, shots, steps,
    now_h, prev_h, snap_h, vel_h, rho_h, count, rec_x, rec_y, res,
    out_now_h, out_prev_h, grad,
    fa, fb, snap, rho, vel, buoy, rho_halo, buoy_halo, halo, coef, img, plane_src,
    pair_in, pair_sum, chain_in,
    load_sem, own_sem, gather_send, gather_recv, edge_send, edge_recv,
    halo_send, halo_recv, pair_send, pair_recv, chain_send, chain_recv, store_sem,
):
    planes, width_x, width_y = fa.shape
    rows = rho_h.shape[1]
    chain = shots // 2
    d, s = lax.axis_index("depth"), lax.axis_index("shots")
    z, c = s // 2, s % 2
    other = 2 * z + (1 - c)
    has_below, has_above = d > 0, d < depths - 1

    loads = [
        pltpu.make_async_copy(now_h, fa, load_sem.at[0]),
        pltpu.make_async_copy(prev_h, fb, load_sem.at[1]),
        pltpu.make_async_copy(snap_h, snap, load_sem.at[2]),
    ]

    def slab(ref, index):
        return ref.at[:, pl.ds(pl.multiple_of(index * rows, 8), rows), :]

    model = (rho, vel)
    model_h = (rho_h, vel_h)
    own = [pltpu.make_async_copy(model_h[a], slab(model[a], s), own_sem.at[a]) for a in range(2)]

    barrier = pltpu.get_barrier_semaphore()
    pl.semaphore_signal(barrier, inc=1, device_id=(d, other), device_id_type=MESH)
    for j in range(1, chain):
        peer = 2 * ((z + j) % chain) + c
        pl.semaphore_signal(barrier, inc=1, device_id=(d, peer), device_id_type=MESH)

    @pl.when(has_below)
    def _():
        pl.semaphore_signal(barrier, inc=1, device_id=(d - 1, s), device_id_type=MESH)

    @pl.when(has_above)
    def _():
        pl.semaphore_signal(barrier, inc=1, device_id=(d + 1, s), device_id_type=MESH)

    for copy in own + loads:
        copy.start()
    pl.semaphore_wait(barrier, chain + has_below.astype(jnp.int32) + has_above.astype(jnp.int32))

    def send(a, index, way, first=False):
        target = (2 * (z - 1) + c, 2 * (z + 1) + c, other)[way]
        return pltpu.make_async_remote_copy(
            src_ref=model_h[a] if first else slab(model[a], index),
            dst_ref=slab(model[a], index),
            send_sem=gather_send.at[a, index, way],
            recv_sem=gather_recv.at[a, index],
            device_id=(d, target), device_id_type=MESH,
        )

    def arrived(a, index):
        send(a, index, 2).wait_recv()

    has_left, has_right = z > 0, z < chain - 1
    for a in range(2):
        pl.when(has_left)(lambda a=a: send(a, s, 0, True).start())
        pl.when(has_right)(lambda a=a: send(a, s, 1, True).start())
    for a in range(2):
        send(a, s, 2, True).start()

    def edge(step, side, src):
        return pltpu.make_async_remote_copy(
            src_ref=src, dst_ref=halo.at[step, pl.ds(1 - side, 1)],
            send_sem=halo_send.at[step, side], recv_sem=halo_recv.at[step, 1 - side],
            device_id=(d - 1 if side == 0 else d + 1, s), device_id_type=MESH,
        )

    def edge_src(field, side):
        return field.at[pl.ds(0 if side == 0 else planes - 1, 1)]

    exists = (has_below, has_above)
    for side in range(2):
        pl.when(exists[side])(lambda side=side: edge(0, side, edge_src(now_h, side)).start())

        @pl.when(jnp.logical_not(exists[side]))
        def _(side=side):
            rho_halo[side] = jnp.ones((width_x, width_y), jnp.float32)
            for step in range(steps):
                halo[step, side] = jnp.zeros((width_x, width_y), jnp.float32)

    nrec = rec_x.shape[1]
    spot_x = lax.broadcasted_iota(jnp.int32, (width_x, nrec), 0) == rec_x[...]
    spot_y = (lax.broadcasted_iota(jnp.int32, (width_y, nrec), 0) == rec_y[...]).astype(jnp.float32)
    scale = jnp.where(d == 0, 0.08, 0.0).astype(jnp.float32)
    for t in range(steps):
        amounts = jnp.where(spot_x, res[t : t + 1, :], 0.0)
        plane_src[t] = scale * lax.dot_general(
            amounts, spot_y, (((1,), (1,)), ((), ())),
            precision=lax.Precision.HIGHEST, preferred_element_type=jnp.float32,
        )

    for k in range(1, chain):
        for a in range(2):

            @pl.when(z - k >= 0)
            def _(a=a, k=k):
                index = 2 * (z - k) + c
                arrived(a, index)
                pl.when(has_right)(lambda: send(a, index, 1).start())
                send(a, index, 2).start()

            @pl.when(z + k <= chain - 1)
            def _(a=a, k=k):
                index = 2 * (z + k) + c
                arrived(a, index)
                pl.when(has_left)(lambda: send(a, index, 0).start())
                send(a, index, 2).start()

    for copy in own:
        copy.wait()
    for a in range(2):
        for j in range(chain):
            arrived(a, 2 * j + (1 - c))

    def rho_edge(side):
        return pltpu.make_async_remote_copy(
            src_ref=edge_src(rho, side), dst_ref=rho_halo.at[pl.ds(1 - side, 1)],
            send_sem=edge_send.at[side], recv_sem=edge_recv.at[1 - side],
            device_id=(d - 1 if side == 0 else d + 1, s), device_id_type=MESH,
        )

    for side in range(2):
        pl.when(exists[side])(lambda side=side: rho_edge(side).start())

    row = lax.broadcasted_iota(jnp.int32, (width_x, width_y), 0)
    col = lax.broadcasted_iota(jnp.int32, (width_x, width_y), 1)

    @pl.loop(0, planes)
    def _(i):
        buoy[i] = 1.0 / rho[i]

    def coefficients(i, below, above):
        b = buoy[i]
        r, v = rho[i], vel[i]
        k = (0.08 * 0.5) * (r * v * v)
        kb = k * b
        total = jnp.zeros_like(b)
        for n, (axis, shift, size, at, last) in enumerate((
            (0, width_x - 1, width_x, row, width_x - 1),
            (0, 1, width_x, row, 0),
            (1, width_y - 1, width_y, col, width_y - 1),
            (1, 1, width_y, col, 0),
        )):
            outside = at == last
            w = kb + k * jnp.where(outside, 0.0, pltpu.roll(b, shift, axis))
            total = total + w
            coef[n, i] = jnp.where(outside, 0.0, w)
        for n, near in ((4, below), (5, above)):
            w = kb + k * near
            total = total + w
            coef[n, i] = w
        coef[6, i] = 2.0 - total

    @pl.loop(1, planes - 1)
    def _(i):
        coefficients(i, buoy[i - 1], buoy[i + 1])

    for side in range(2):
        pl.when(exists[side])(lambda side=side: rho_edge(1 - side).wait_recv())
        buoy_halo[side] = jnp.where(exists[side], 1.0 / rho_halo[side], 0.0)
    coefficients(0, buoy_halo[0], buoy[1])
    coefficients(planes - 1, buoy[planes - 2], buoy_halo[1])

    for copy in loads:
        copy.wait()

    weight = count[0].astype(jnp.float32)
    cur, old = fa, fb
    for step in range(steps):
        t = steps - 1 - step

        def advance(i, below, above, source=None, cur=cur, old=old, step=step, t=t):
            p = cur[i]
            new = coef[6, i] * p - old[i]
            if source is not None:
                new = new + source
            new = new + coef[4, i] * below + coef[5, i] * above
            new = new + coef[0, i] * pltpu.roll(p, width_x - 1, 0)
            new = new + coef[1, i] * pltpu.roll(p, 1, 0)
            new = new + coef[2, i] * pltpu.roll(p, width_y - 1, 1)
            new = new + coef[3, i] * pltpu.roll(p, 1, 1)
            old[i] = new
            term = snap[t, i].astype(jnp.float32) * new
            if step > 0:
                term = img[i] + term
            img[i] = weight * term if step == steps - 1 else term

        for side in range(2):
            pl.when(exists[side])(
                lambda side=side, step=step: edge(step, 1 - side, edge_src(now_h, side)).wait_recv()
            )
        advance(0, halo[step, 0], cur[1])
        advance(planes - 1, cur[planes - 2], halo[step, 1])
        if step < steps - 1:
            for side in range(2):
                pl.when(exists[side])(
                    lambda side=side, step=step, old=old: edge(step + 1, side, edge_src(old, side)).start()
                )
        advance(1, cur[0], cur[2])
        advance(2, cur[1], cur[3], plane_src[t])

        @pl.loop(3, planes - 1)
        def _(i, advance=advance, cur=cur):
            advance(i, cur[i - 1], cur[i + 1])

        if step < steps - 1:
            for side in range(2):
                pl.when(exists[side])(
                    lambda side=side, step=step, old=old: edge(step + 1, side, edge_src(old, side)).wait_send()
                )
        cur, old = old, cur

    def to_pair(j):
        return pltpu.make_async_remote_copy(
            src_ref=slab(img, 2 * j + (1 - c)), dst_ref=pair_in.at[j],
            send_sem=pair_send.at[j], recv_sem=pair_recv.at[j],
            device_id=(d, other), device_id_type=MESH,
        )

    def to_owner(j, slot):
        return pltpu.make_async_remote_copy(
            src_ref=pair_sum.at[j], dst_ref=chain_in.at[slot],
            send_sem=chain_send.at[j], recv_sem=chain_recv.at[slot],
            device_id=(d, 2 * j + c), device_id_type=MESH,
        )

    order = [(z + j) % chain for j in range(1, chain + 1)]
    for j in order:
        to_pair(j).start()
    stores = [
        pltpu.make_async_copy(cur, out_now_h, store_sem.at[0]),
        pltpu.make_async_copy(old, out_prev_h, store_sem.at[1]),
    ]
    for copy in stores:
        copy.start()
    for n, j in enumerate(order):
        to_pair(j).wait_recv()
        at = pl.ds(pl.multiple_of((2 * j + c) * rows, 8), rows)
        pair_sum[j] = img[:, at, :] + pair_in[j]
        if n < chain - 1:
            to_owner(j, z).start()
    mine = pl.ds(pl.multiple_of(s * rows, 8), rows)
    factor = (2.0 / (4.0 * shots)) * (rho[:, mine, :] * vel[:, mine, :])
    total = pair_sum[z]
    for n in range(1, chain):
        j = (z - n + chain) % chain
        to_owner(j, j).wait_recv()
        total = total + chain_in[j]
    grad[...] = factor * total

    for copy in stores:
        copy.wait()
    for j in order:
        to_pair(j).wait_send()
    for j in order[:-1]:
        to_owner(j, z).wait_send()
    for side in range(2):

        @pl.when(exists[side])
        def _(side=side):
            edge(0, side, edge_src(now_h, side)).wait_send()
            rho_edge(side).wait_send()

    for a in range(2):
        pl.when(has_left)(lambda a=a: send(a, s, 0, True).wait_send())
        pl.when(has_right)(lambda a=a: send(a, s, 1, True).wait_send())
        send(a, s, 2, True).wait_send()
        for k in range(1, chain):

            @pl.when(z - k >= 0)
            def _(a=a, k=k):
                index = 2 * (z - k) + c
                pl.when(has_right)(lambda: send(a, index, 1).wait_send())
                send(a, index, 2).wait_send()

            @pl.when(z + k <= chain - 1)
            def _(a=a, k=k):
                index = 2 * (z + k) + c
                pl.when(has_left)(lambda: send(a, index, 0).wait_send())
                send(a, index, 2).wait_send()


def fused(adj_now, adj_prev, fwd_snap, velocity, density, shot_count, rec_x, rec_y, residual):
    depths, shots = lax.axis_size("depth"), lax.axis_size("shots")
    field = adj_now.shape[1:]
    planes, width_x, width_y = field
    steps = fwd_snap.shape[1]
    shard = velocity.shape
    chain = shots // 2
    anywhere = pl.BlockSpec(memory_space=pl.ANY)
    vmem = pl.BlockSpec(memory_space=pltpu.VMEM)
    f32 = jnp.float32
    dma = pltpu.SemaphoreType.DMA
    now, prev, grad = pl.pallas_call(
        functools.partial(kernel, depths, shots, steps),
        out_shape=(
            jax.ShapeDtypeStruct(field, f32),
            jax.ShapeDtypeStruct(field, f32),
            jax.ShapeDtypeStruct(shard, f32),
        ),
        in_specs=[anywhere] * 5 + [pl.BlockSpec(memory_space=pltpu.SMEM)] + [vmem] * 3,
        out_specs=(anywhere, anywhere, vmem),
        scratch_shapes=[
            pltpu.VMEM(field, f32),
            pltpu.VMEM(field, f32),
            pltpu.VMEM((steps,) + field, fwd_snap.dtype),
            pltpu.VMEM(field, f32),
            pltpu.VMEM(field, f32),
            pltpu.VMEM(field, f32),
            pltpu.VMEM((2, width_x, width_y), f32),
            pltpu.VMEM((2, width_x, width_y), f32),
            pltpu.VMEM((steps, 2, width_x, width_y), f32),
            pltpu.VMEM((7,) + field, f32),
            pltpu.VMEM(field, f32),
            pltpu.VMEM((steps, width_x, width_y), f32),
            pltpu.VMEM((chain,) + shard, f32),
            pltpu.VMEM((chain,) + shard, f32),
            pltpu.VMEM((chain,) + shard, f32),
            dma((3,)), dma((2,)), dma((2, shots, 3)), dma((2, shots)), dma((2,)), dma((2,)),
            dma((steps, 2)), dma((steps, 2)), dma((chain,)), dma((chain,)), dma((chain,)), dma((chain,)),
            dma((2,)),
        ],
        compiler_params=pltpu.CompilerParams(
            collective_id=0, has_side_effects=True, vmem_limit_bytes=40 << 20
        ),
        name="adjoint_steps",
    )(
        adj_now[0], adj_prev[0], fwd_snap[0], velocity, density, shot_count, rec_x, rec_y, residual[0]
    )
    return now[None], prev[None], grad


def chosen(*args):
    planes, rows = args[3].shape[:2]
    if rows % 8 == 0 and planes > 4 and lax.axis_size("shots") % 2 == 0:
        return fused(*args)
    return body(*args)


def solution(mesh):
    in_specs = (
        P("shots", "depth", None, None),
        P("shots", "depth", None, None),
        P("shots", None, "depth", None, None),
        P("depth", "shots", None),
        P("depth", "shots", None),
        P("shots"),
        P("shots", None),
        P("shots", None),
        P("shots", None, None),
    )
    out_specs = (
        P("shots", "depth", None, None),
        P("shots", "depth", None, None),
        P("depth", "shots", None),
    )
    return jax.shard_map(chosen, mesh=mesh, in_specs=in_specs, out_specs=out_specs, check_vma=False)
```

```python
import functools
import jax
import jax.numpy as jnp
from jax import lax
from jax.experimental import pallas as pl
from jax.experimental.pallas import tpu as pltpu
from jax.sharding import PartitionSpec as P


def with_halo(shard, sides, width):
    for axis, dim in sides:
        peers, length = (lax.axis_size(axis), shard.shape[dim])
        up = [(i, (i + 1) % peers) for i in range(peers - 1)]
        down = [(j, i) for i, j in up]
        last = lax.slice_in_dim(shard, length - width, length, axis=dim)
        first = lax.slice_in_dim(shard, 0, width, axis=dim)
        before = lax.ppermute(last, axis, up)
        after = lax.ppermute(first, axis, down)
        shard = jnp.concatenate([before, shard, after], axis=dim)
    return shard


def operate(field, buoy):
    padded = jnp.pad(field, 1)
    bpad = jnp.pad(buoy, 1)
    total = jnp.zeros_like(field)
    for axis in range(3):
        center = [slice(1, -1)] * 3
        ahead = list(center)
        behind = list(center)
        ahead[axis] = slice(2, None)
        behind[axis] = slice(0, -2)
        pc, pa, pb = (padded[tuple(center)], padded[tuple(ahead)], padded[tuple(behind)])
        bc, ba, bb = (bpad[tuple(center)], bpad[tuple(ahead)], bpad[tuple(behind)])
        total = total + 0.5 * (bc + ba) * (pa - pc) - 0.5 * (bb + bc) * (pc - pb)
    return total


def source_plane(rows_x, rows_y, amounts, width_x, width_y):
    onehot_x = (rows_x[:, None] == jnp.arange(width_x, dtype=jnp.int32)[None, :]).astype(
        jnp.float32
    )
    onehot_y = (rows_y[:, None] == jnp.arange(width_y, dtype=jnp.int32)[None, :]).astype(
        jnp.float32
    )
    return jnp.dot((onehot_x * amounts[:, None]).T, onehot_y, precision=lax.Precision.HIGHEST)


def body(adj_now, adj_prev, fwd_snap, velocity, density, shot_count, rec_x, rec_y, residual):
    depth_planes = adj_now.shape[1]
    width_x = adj_now.shape[2]
    width_y = adj_now.shape[3]
    steps = fwd_snap.shape[1]
    groups = lax.axis_size("shots")
    width = 1
    vel_all, rho_all = (
        lax.all_gather(velocity, "shots", axis=1, tiled=True),
        lax.all_gather(density, "shots", axis=1, tiled=True),
    )
    packed = jnp.stack([rho_all * vel_all * vel_all, 1.0 / rho_all])
    extended = with_halo(packed, (("depth", 1),), width)
    buoy_ext = extended[1]
    first = lax.axis_index("depth") * depth_planes
    snaps = fwd_snap[0]
    rows_x = rec_x[0]
    rows_y = rec_y[0]
    image = jnp.zeros((depth_planes, width_x, width_y), jnp.float32)
    kappa_ext = extended[0, width : width + depth_planes]
    global_plane = first + jnp.arange(depth_planes, dtype=jnp.int32)
    at_receivers = (global_plane == 2).astype(jnp.float32)[:, None, None]
    current = adj_now[0]
    older = adj_prev[0]
    for step in range(steps):
        moment = steps - 1 - step
        rimmed_field = with_halo(current[None], (("depth", 1),), 1)[0]
        plane = source_plane(rows_x, rows_y, residual[0, moment], width_x, width_y)
        spread = operate(rimmed_field, buoy_ext)[1:-1]
        newer = (
            2.0 * current - older + 0.08 * kappa_ext * spread + 0.08 * at_receivers * plane[None]
        )
        image = image + snaps[moment].astype(jnp.float32) * newer
        older = current
        current = newer
    weighted = shot_count[0].astype(jnp.float32) * image
    summed = lax.psum_scatter(weighted, "shots", scatter_dimension=1, tiled=True)
    grad_vel = 2.0 * density * velocity * summed / (4.0 * groups)
    return (current[None], older[None], grad_vel)


MESH = pl.DeviceIdType.MESH


def kernel(
    depths, shots, steps,
    now_h, prev_h, snap_h, vel_h, rho_h, count, rec_x_h, rec_y_h, res_h,
    out_now_h, out_prev_h, grad,
    rec_x, rec_y, res, fa, fb, snap, rho, vel, buoy, rho_halo, buoy_halo, halo, coef, img, plane_src,
    pair_in, pair_sum, chain_in,
    load_sem, own_sem, gather_send, gather_recv, edge_send, edge_recv,
    halo_send, halo_recv, pair_send, pair_recv, chain_send, chain_recv, store_sem, small_sem,
):
    planes, width_x, width_y = fa.shape
    rows = rho_h.shape[1]
    chain = shots // 2
    d, s = lax.axis_index("depth"), lax.axis_index("shots")
    z, c = s // 2, s % 2
    other = 2 * z + (1 - c)
    has_below, has_above = d > 0, d < depths - 1

    loads = [
        pltpu.make_async_copy(now_h, fa, load_sem.at[0]),
        pltpu.make_async_copy(prev_h, fb, load_sem.at[1]),
        pltpu.make_async_copy(snap_h, snap, load_sem.at[2]),
    ]
    small = [
        pltpu.make_async_copy(a, b, small_sem.at[n])
        for n, (a, b) in enumerate(((rec_x_h, rec_x), (rec_y_h, rec_y), (res_h, res)))
    ]

    def slab(ref, index):
        return ref.at[:, pl.ds(pl.multiple_of(index * rows, 8), rows), :]

    model = (rho, vel)
    model_h = (rho_h, vel_h)
    own = [pltpu.make_async_copy(model_h[a], slab(model[a], s), own_sem.at[a]) for a in range(2)]

    barrier = pltpu.get_barrier_semaphore()
    pl.semaphore_signal(barrier, inc=1, device_id=(d, other), device_id_type=MESH)
    for j in range(1, chain):
        peer = 2 * ((z + j) % chain) + c
        pl.semaphore_signal(barrier, inc=1, device_id=(d, peer), device_id_type=MESH)

    @pl.when(has_below)
    def _():
        pl.semaphore_signal(barrier, inc=1, device_id=(d - 1, s), device_id_type=MESH)

    @pl.when(has_above)
    def _():
        pl.semaphore_signal(barrier, inc=1, device_id=(d + 1, s), device_id_type=MESH)

    for copy in own + small + loads:
        copy.start()
    pl.semaphore_wait(barrier, chain + has_below.astype(jnp.int32) + has_above.astype(jnp.int32))

    def send(a, index, way, first=False):
        target = (2 * (z - 1) + c, 2 * (z + 1) + c, other)[way]
        return pltpu.make_async_remote_copy(
            src_ref=model_h[a] if first else slab(model[a], index),
            dst_ref=slab(model[a], index),
            send_sem=gather_send.at[a, index, way],
            recv_sem=gather_recv.at[a, index],
            device_id=(d, target), device_id_type=MESH,
        )

    def arrived(a, index):
        send(a, index, 2).wait_recv()

    has_left, has_right = z > 0, z < chain - 1
    for a in range(2):
        pl.when(has_left)(lambda a=a: send(a, s, 0, True).start())
        pl.when(has_right)(lambda a=a: send(a, s, 1, True).start())
    for a in range(2):
        send(a, s, 2, True).start()

    def edge(step, side, src):
        return pltpu.make_async_remote_copy(
            src_ref=src, dst_ref=halo.at[step, pl.ds(1 - side, 1)],
            send_sem=halo_send.at[step, side], recv_sem=halo_recv.at[step, 1 - side],
            device_id=(d - 1 if side == 0 else d + 1, s), device_id_type=MESH,
        )

    def edge_src(field, side):
        return field.at[pl.ds(0 if side == 0 else planes - 1, 1)]

    exists = (has_below, has_above)
    for side in range(2):
        pl.when(exists[side])(lambda side=side: edge(0, side, edge_src(now_h, side)).start())

        @pl.when(jnp.logical_not(exists[side]))
        def _(side=side):
            rho_halo[side] = jnp.ones((width_x, width_y), jnp.float32)
            for step in range(steps):
                halo[step, side] = jnp.zeros((width_x, width_y), jnp.float32)

    for copy in small:
        copy.wait()
    nrec = rec_x.shape[1]
    spot_x = lax.broadcasted_iota(jnp.int32, (width_x, nrec), 0) == rec_x[...]
    spot_y = (lax.broadcasted_iota(jnp.int32, (width_y, nrec), 0) == rec_y[...]).astype(jnp.float32)
    scale = jnp.where(d == 0, 0.08, 0.0).astype(jnp.float32)
    for t in range(steps):
        amounts = jnp.where(spot_x, res[t : t + 1, :], 0.0)
        plane_src[t] = scale * lax.dot_general(
            amounts, spot_y, (((1,), (1,)), ((), ())),
            precision=lax.Precision.HIGHEST, preferred_element_type=jnp.float32,
        )

    for k in range(1, chain):
        for a in range(2):

            @pl.when(z - k >= 0)
            def _(a=a, k=k):
                index = 2 * (z - k) + c
                arrived(a, index)
                pl.when(has_right)(lambda: send(a, index, 1).start())
                send(a, index, 2).start()

            @pl.when(z + k <= chain - 1)
            def _(a=a, k=k):
                index = 2 * (z + k) + c
                arrived(a, index)
                pl.when(has_left)(lambda: send(a, index, 0).start())
                send(a, index, 2).start()

    for copy in own:
        copy.wait()
    for a in range(2):
        for j in range(chain):
            arrived(a, 2 * j + (1 - c))

    def rho_edge(side):
        return pltpu.make_async_remote_copy(
            src_ref=edge_src(rho, side), dst_ref=rho_halo.at[pl.ds(1 - side, 1)],
            send_sem=edge_send.at[side], recv_sem=edge_recv.at[1 - side],
            device_id=(d - 1 if side == 0 else d + 1, s), device_id_type=MESH,
        )

    for side in range(2):
        pl.when(exists[side])(lambda side=side: rho_edge(side).start())

    row = lax.broadcasted_iota(jnp.int32, (width_x, width_y), 0)
    col = lax.broadcasted_iota(jnp.int32, (width_x, width_y), 1)

    @pl.loop(0, planes)
    def _(i):
        buoy[i] = 1.0 / rho[i]

    def coefficients(i, below, above):
        b = buoy[i]
        r, v = rho[i], vel[i]
        k = (0.08 * 0.5) * (r * v * v)
        kb = k * b
        total = jnp.zeros_like(b)
        for n, (axis, shift, size, at, last) in enumerate((
            (0, width_x - 1, width_x, row, width_x - 1),
            (0, 1, width_x, row, 0),
            (1, width_y - 1, width_y, col, width_y - 1),
            (1, 1, width_y, col, 0),
        )):
            outside = at == last
            w = kb + k * jnp.where(outside, 0.0, pltpu.roll(b, shift, axis))
            total = total + w
            coef[n, i] = jnp.where(outside, 0.0, w)
        for n, near in ((4, below), (5, above)):
            w = kb + k * near
            total = total + w
            coef[n, i] = w
        coef[6, i] = 2.0 - total

    @pl.loop(1, planes - 1)
    def _(i):
        coefficients(i, buoy[i - 1], buoy[i + 1])

    for side in range(2):
        pl.when(exists[side])(lambda side=side: rho_edge(1 - side).wait_recv())
        buoy_halo[side] = jnp.where(exists[side], 1.0 / rho_halo[side], 0.0)
    coefficients(0, buoy_halo[0], buoy[1])
    coefficients(planes - 1, buoy[planes - 2], buoy_halo[1])

    for copy in loads:
        copy.wait()

    weight = count[0].astype(jnp.float32)
    cur, old = fa, fb
    for step in range(steps):
        t = steps - 1 - step

        def advance(i, below, above, source=None, cur=cur, old=old, step=step, t=t):
            p = cur[i]
            new = coef[6, i] * p - old[i]
            if source is not None:
                new = new + source
            new = new + coef[4, i] * below + coef[5, i] * above
            new = new + coef[0, i] * pltpu.roll(p, width_x - 1, 0)
            new = new + coef[1, i] * pltpu.roll(p, 1, 0)
            new = new + coef[2, i] * pltpu.roll(p, width_y - 1, 1)
            new = new + coef[3, i] * pltpu.roll(p, 1, 1)
            old[i] = new
            term = snap[t, i].astype(jnp.float32) * new
            if step > 0:
                term = img[i] + term
            img[i] = weight * term if step == steps - 1 else term

        for side in range(2):
            pl.when(exists[side])(
                lambda side=side, step=step: edge(step, 1 - side, edge_src(now_h, side)).wait_recv()
            )
        advance(0, halo[step, 0], cur[1])
        advance(planes - 1, cur[planes - 2], halo[step, 1])
        if step < steps - 1:
            for side in range(2):
                pl.when(exists[side])(
                    lambda side=side, step=step, old=old: edge(step + 1, side, edge_src(old, side)).start()
                )
        advance(1, cur[0], cur[2])
        advance(2, cur[1], cur[3], plane_src[t])

        @pl.loop(3, planes - 1)
        def _(i, advance=advance, cur=cur):
            advance(i, cur[i - 1], cur[i + 1])

        if step < steps - 1:
            for side in range(2):
                pl.when(exists[side])(
                    lambda side=side, step=step, old=old: edge(step + 1, side, edge_src(old, side)).wait_send()
                )
        cur, old = old, cur

    def to_pair(j):
        return pltpu.make_async_remote_copy(
            src_ref=slab(img, 2 * j + (1 - c)), dst_ref=pair_in.at[j],
            send_sem=pair_send.at[j], recv_sem=pair_recv.at[j],
            device_id=(d, other), device_id_type=MESH,
        )

    def to_owner(j, slot):
        return pltpu.make_async_remote_copy(
            src_ref=pair_sum.at[j], dst_ref=chain_in.at[slot],
            send_sem=chain_send.at[j], recv_sem=chain_recv.at[slot],
            device_id=(d, 2 * j + c), device_id_type=MESH,
        )

    order = [(z + j) % chain for j in range(1, chain + 1)]
    for j in order:
        to_pair(j).start()
    stores = [
        pltpu.make_async_copy(cur, out_now_h, store_sem.at[0]),
        pltpu.make_async_copy(old, out_prev_h, store_sem.at[1]),
    ]
    for copy in stores:
        copy.start()
    for n, j in enumerate(order):
        to_pair(j).wait_recv()
        at = pl.ds(pl.multiple_of((2 * j + c) * rows, 8), rows)
        pair_sum[j] = img[:, at, :] + pair_in[j]
        if n < chain - 1:
            to_owner(j, z).start()
    mine = pl.ds(pl.multiple_of(s * rows, 8), rows)
    factor = (2.0 / (4.0 * shots)) * (rho[:, mine, :] * vel[:, mine, :])
    total = pair_sum[z]
    for n in range(1, chain):
        j = (z - n + chain) % chain
        to_owner(j, j).wait_recv()
        total = total + chain_in[j]
    grad[...] = factor * total

    for copy in stores:
        copy.wait()
    for j in order:
        to_pair(j).wait_send()
    for j in order[:-1]:
        to_owner(j, z).wait_send()
    for side in range(2):

        @pl.when(exists[side])
        def _(side=side):
            edge(0, side, edge_src(now_h, side)).wait_send()
            rho_edge(side).wait_send()

    for a in range(2):
        pl.when(has_left)(lambda a=a: send(a, s, 0, True).wait_send())
        pl.when(has_right)(lambda a=a: send(a, s, 1, True).wait_send())
        send(a, s, 2, True).wait_send()
        for k in range(1, chain):

            @pl.when(z - k >= 0)
            def _(a=a, k=k):
                index = 2 * (z - k) + c
                pl.when(has_right)(lambda: send(a, index, 1).wait_send())
                send(a, index, 2).wait_send()

            @pl.when(z + k <= chain - 1)
            def _(a=a, k=k):
                index = 2 * (z + k) + c
                pl.when(has_left)(lambda: send(a, index, 0).wait_send())
                send(a, index, 2).wait_send()


def fused(adj_now, adj_prev, fwd_snap, velocity, density, shot_count, rec_x, rec_y, residual):
    depths, shots = lax.axis_size("depth"), lax.axis_size("shots")
    field = adj_now.shape[1:]
    planes, width_x, width_y = field
    steps = fwd_snap.shape[1]
    shard = velocity.shape
    chain = shots // 2
    anywhere = pl.BlockSpec(memory_space=pl.ANY)
    vmem = pl.BlockSpec(memory_space=pltpu.VMEM)
    f32 = jnp.float32
    dma = pltpu.SemaphoreType.DMA
    now, prev, grad = pl.pallas_call(
        functools.partial(kernel, depths, shots, steps),
        out_shape=(
            jax.ShapeDtypeStruct(field, f32),
            jax.ShapeDtypeStruct(field, f32),
            jax.ShapeDtypeStruct(shard, f32),
        ),
        in_specs=[anywhere] * 5 + [pl.BlockSpec(memory_space=pltpu.SMEM)] + [anywhere] * 3,
        out_specs=(anywhere, anywhere, vmem),
        scratch_shapes=[
            pltpu.VMEM(rec_x.shape, rec_x.dtype),
            pltpu.VMEM(rec_y.shape, rec_y.dtype),
            pltpu.VMEM(residual.shape[1:], f32),
            pltpu.VMEM(field, f32),
            pltpu.VMEM(field, f32),
            pltpu.VMEM((steps,) + field, fwd_snap.dtype),
            pltpu.VMEM(field, f32),
            pltpu.VMEM(field, f32),
            pltpu.VMEM(field, f32),
            pltpu.VMEM((2, width_x, width_y), f32),
            pltpu.VMEM((2, width_x, width_y), f32),
            pltpu.VMEM((steps, 2, width_x, width_y), f32),
            pltpu.VMEM((7,) + field, f32),
            pltpu.VMEM(field, f32),
            pltpu.VMEM((steps, width_x, width_y), f32),
            pltpu.VMEM((chain,) + shard, f32),
            pltpu.VMEM((chain,) + shard, f32),
            pltpu.VMEM((chain,) + shard, f32),
            dma((3,)), dma((2,)), dma((2, shots, 3)), dma((2, shots)), dma((2,)), dma((2,)),
            dma((steps, 2)), dma((steps, 2)), dma((chain,)), dma((chain,)), dma((chain,)), dma((chain,)),
            dma((2,)), dma((3,)),
        ],
        compiler_params=pltpu.CompilerParams(
            collective_id=0, has_side_effects=True, vmem_limit_bytes=60 << 20
        ),
        name="adjoint_steps",
    )(
        adj_now[0], adj_prev[0], fwd_snap[0], velocity, density, shot_count, rec_x, rec_y, residual[0]
    )
    return now[None], prev[None], grad


def chosen(*args):
    planes, rows = args[3].shape[:2]
    if rows % 8 == 0 and planes > 4 and lax.axis_size("shots") % 2 == 0:
        return fused(*args)
    return body(*args)


def solution(mesh):
    in_specs = (
        P("shots", "depth", None, None),
        P("shots", "depth", None, None),
        P("shots", None, "depth", None, None),
        P("depth", "shots", None),
        P("depth", "shots", None),
        P("shots"),
        P("shots", None),
        P("shots", None),
        P("shots", None, None),
    )
    out_specs = (
        P("shots", "depth", None, None),
        P("shots", "depth", None, None),
        P("depth", "shots", None),
    )
    return jax.shard_map(chosen, mesh=mesh, in_specs=in_specs, out_specs=out_specs, check_vma=False)
```

```python
import functools
import jax
import jax.numpy as jnp
from jax import lax
from jax.experimental import pallas as pl
from jax.experimental.pallas import tpu as pltpu
from jax.sharding import PartitionSpec as P


def with_halo(shard, sides, width):
    for axis, dim in sides:
        peers, length = (lax.axis_size(axis), shard.shape[dim])
        up = [(i, (i + 1) % peers) for i in range(peers - 1)]
        down = [(j, i) for i, j in up]
        last = lax.slice_in_dim(shard, length - width, length, axis=dim)
        first = lax.slice_in_dim(shard, 0, width, axis=dim)
        before = lax.ppermute(last, axis, up)
        after = lax.ppermute(first, axis, down)
        shard = jnp.concatenate([before, shard, after], axis=dim)
    return shard


def operate(field, buoy):
    padded = jnp.pad(field, 1)
    bpad = jnp.pad(buoy, 1)
    total = jnp.zeros_like(field)
    for axis in range(3):
        center = [slice(1, -1)] * 3
        ahead = list(center)
        behind = list(center)
        ahead[axis] = slice(2, None)
        behind[axis] = slice(0, -2)
        pc, pa, pb = (padded[tuple(center)], padded[tuple(ahead)], padded[tuple(behind)])
        bc, ba, bb = (bpad[tuple(center)], bpad[tuple(ahead)], bpad[tuple(behind)])
        total = total + 0.5 * (bc + ba) * (pa - pc) - 0.5 * (bb + bc) * (pc - pb)
    return total


def source_plane(rows_x, rows_y, amounts, width_x, width_y):
    onehot_x = (rows_x[:, None] == jnp.arange(width_x, dtype=jnp.int32)[None, :]).astype(
        jnp.float32
    )
    onehot_y = (rows_y[:, None] == jnp.arange(width_y, dtype=jnp.int32)[None, :]).astype(
        jnp.float32
    )
    return jnp.dot((onehot_x * amounts[:, None]).T, onehot_y, precision=lax.Precision.HIGHEST)


def body(adj_now, adj_prev, fwd_snap, velocity, density, shot_count, rec_x, rec_y, residual):
    depth_planes = adj_now.shape[1]
    width_x = adj_now.shape[2]
    width_y = adj_now.shape[3]
    steps = fwd_snap.shape[1]
    groups = lax.axis_size("shots")
    width = 1
    vel_all, rho_all = (
        lax.all_gather(velocity, "shots", axis=1, tiled=True),
        lax.all_gather(density, "shots", axis=1, tiled=True),
    )
    packed = jnp.stack([rho_all * vel_all * vel_all, 1.0 / rho_all])
    extended = with_halo(packed, (("depth", 1),), width)
    buoy_ext = extended[1]
    first = lax.axis_index("depth") * depth_planes
    snaps = fwd_snap[0]
    rows_x = rec_x[0]
    rows_y = rec_y[0]
    image = jnp.zeros((depth_planes, width_x, width_y), jnp.float32)
    kappa_ext = extended[0, width : width + depth_planes]
    global_plane = first + jnp.arange(depth_planes, dtype=jnp.int32)
    at_receivers = (global_plane == 2).astype(jnp.float32)[:, None, None]
    current = adj_now[0]
    older = adj_prev[0]
    for step in range(steps):
        moment = steps - 1 - step
        rimmed_field = with_halo(current[None], (("depth", 1),), 1)[0]
        plane = source_plane(rows_x, rows_y, residual[0, moment], width_x, width_y)
        spread = operate(rimmed_field, buoy_ext)[1:-1]
        newer = (
            2.0 * current - older + 0.08 * kappa_ext * spread + 0.08 * at_receivers * plane[None]
        )
        image = image + snaps[moment].astype(jnp.float32) * newer
        older = current
        current = newer
    weighted = shot_count[0].astype(jnp.float32) * image
    summed = lax.psum_scatter(weighted, "shots", scatter_dimension=1, tiled=True)
    grad_vel = 2.0 * density * velocity * summed / (4.0 * groups)
    return (current[None], older[None], grad_vel)


MESH = pl.DeviceIdType.MESH


def kernel(
    depths, shots, steps,
    now_h, prev_h, snap_h, vel_h, rho_h, count, rec_x_h, rec_y_h, res_h,
    out_now_h, out_prev_h, grad,
    rec_x, rec_y, res, fa, fb, snap, rho, vel, buoy, rho_halo, buoy_halo, halo, coef, img, plane_src,
    pair_in, pair_sum, chain_in,
    load_sem, own_sem, gather_send, gather_recv, edge_send, edge_recv,
    halo_send, halo_recv, pair_send, pair_recv, chain_send, chain_recv, store_sem, small_sem,
):
    planes, width_x, width_y = fa.shape
    rows = rho_h.shape[1]
    chain = shots // 2
    d, s = lax.axis_index("depth"), lax.axis_index("shots")
    z, c = s // 2, s % 2
    other = 2 * z + (1 - c)
    has_below, has_above = d > 0, d < depths - 1

    loads = [
        pltpu.make_async_copy(now_h, fa, load_sem.at[0]),
        pltpu.make_async_copy(prev_h, fb, load_sem.at[1]),
        pltpu.make_async_copy(snap_h, snap, load_sem.at[2]),
    ]
    small = [
        pltpu.make_async_copy(a, b, small_sem.at[n])
        for n, (a, b) in enumerate(((rec_x_h, rec_x), (rec_y_h, rec_y), (res_h, res)))
    ]

    def slab(ref, index):
        return ref.at[:, pl.ds(pl.multiple_of(index * rows, 8), rows), :]

    model = (rho, vel)
    model_h = (rho_h, vel_h)
    own = [pltpu.make_async_copy(model_h[a], slab(model[a], s), own_sem.at[a]) for a in range(2)]

    barrier = pltpu.get_barrier_semaphore()
    pl.semaphore_signal(barrier, inc=1, device_id=(d, other), device_id_type=MESH)
    for j in range(1, chain):
        peer = 2 * ((z + j) % chain) + c
        pl.semaphore_signal(barrier, inc=1, device_id=(d, peer), device_id_type=MESH)

    @pl.when(has_below)
    def _():
        pl.semaphore_signal(barrier, inc=1, device_id=(d - 1, s), device_id_type=MESH)

    @pl.when(has_above)
    def _():
        pl.semaphore_signal(barrier, inc=1, device_id=(d + 1, s), device_id_type=MESH)

    for copy in own + small + loads:
        copy.start()
    pl.semaphore_wait(barrier, chain + has_below.astype(jnp.int32) + has_above.astype(jnp.int32))

    def send(a, index, way, first=False):
        target = (2 * (z - 1) + c, 2 * (z + 1) + c, other)[way]
        return pltpu.make_async_remote_copy(
            src_ref=model_h[a] if first else slab(model[a], index),
            dst_ref=slab(model[a], index),
            send_sem=gather_send.at[a, index, way],
            recv_sem=gather_recv.at[a, index],
            device_id=(d, target), device_id_type=MESH,
        )

    def arrived(a, index):
        send(a, index, 2).wait_recv()

    has_left, has_right = z > 0, z < chain - 1
    for a in range(2):
        pl.when(has_left)(lambda a=a: send(a, s, 0, True).start())
        pl.when(has_right)(lambda a=a: send(a, s, 1, True).start())
    for a in range(2):
        send(a, s, 2, True).start()

    def edge(step, side, src):
        return pltpu.make_async_remote_copy(
            src_ref=src, dst_ref=halo.at[step, pl.ds(1 - side, 1)],
            send_sem=halo_send.at[step, side], recv_sem=halo_recv.at[step, 1 - side],
            device_id=(d - 1 if side == 0 else d + 1, s), device_id_type=MESH,
        )

    def edge_src(field, side):
        return field.at[pl.ds(0 if side == 0 else planes - 1, 1)]

    exists = (has_below, has_above)
    for side in range(2):
        pl.when(exists[side])(lambda side=side: edge(0, side, edge_src(now_h, side)).start())

        @pl.when(jnp.logical_not(exists[side]))
        def _(side=side):
            rho_halo[side] = jnp.ones((width_x, width_y), jnp.float32)
            for step in range(steps):
                halo[step, side] = jnp.zeros((width_x, width_y), jnp.float32)

    for copy in small:
        copy.wait()
    nrec = rec_x.shape[1]
    spot_x = lax.broadcasted_iota(jnp.int32, (width_x, nrec), 0) == rec_x[...]
    spot_y = (lax.broadcasted_iota(jnp.int32, (width_y, nrec), 0) == rec_y[...]).astype(jnp.float32)
    scale = jnp.where(d == 0, 0.08, 0.0).astype(jnp.float32)
    for t in range(steps):
        amounts = jnp.where(spot_x, res[t : t + 1, :], 0.0)
        plane_src[t] = scale * lax.dot_general(
            amounts, spot_y, (((1,), (1,)), ((), ())),
            precision=lax.Precision.HIGHEST, preferred_element_type=jnp.float32,
        )

    for k in range(1, chain):
        for a in range(2):

            @pl.when(z - k >= 0)
            def _(a=a, k=k):
                index = 2 * (z - k) + c
                arrived(a, index)
                pl.when(has_right)(lambda: send(a, index, 1).start())
                send(a, index, 2).start()

            @pl.when(z + k <= chain - 1)
            def _(a=a, k=k):
                index = 2 * (z + k) + c
                arrived(a, index)
                pl.when(has_left)(lambda: send(a, index, 0).start())
                send(a, index, 2).start()

    for copy in own:
        copy.wait()
    for a in range(2):
        for j in range(chain):
            arrived(a, 2 * j + (1 - c))

    def rho_edge(side):
        return pltpu.make_async_remote_copy(
            src_ref=edge_src(rho, side), dst_ref=rho_halo.at[pl.ds(1 - side, 1)],
            send_sem=edge_send.at[side], recv_sem=edge_recv.at[1 - side],
            device_id=(d - 1 if side == 0 else d + 1, s), device_id_type=MESH,
        )

    for side in range(2):
        pl.when(exists[side])(lambda side=side: rho_edge(side).start())

    row = lax.broadcasted_iota(jnp.int32, (width_x, width_y), 0)
    col = lax.broadcasted_iota(jnp.int32, (width_x, width_y), 1)

    @pl.loop(0, planes)
    def _(i):
        buoy[i] = 1.0 / rho[i]

    def coefficients(i, below, above):
        b = buoy[i]
        r, v = rho[i], vel[i]
        k = (0.08 * 0.5) * (r * v * v)
        kb = k * b
        total = jnp.zeros_like(b)
        for n, (axis, shift, size, at, last) in enumerate((
            (0, width_x - 1, width_x, row, width_x - 1),
            (0, 1, width_x, row, 0),
            (1, width_y - 1, width_y, col, width_y - 1),
            (1, 1, width_y, col, 0),
        )):
            outside = at == last
            w = kb + k * jnp.where(outside, 0.0, pltpu.roll(b, shift, axis))
            total = total + w
            coef[n, i] = jnp.where(outside, 0.0, w)
        for n, near in ((4, below), (5, above)):
            w = kb + k * near
            total = total + w
            coef[n, i] = w
        coef[6, i] = 2.0 - total

    @pl.loop(1, planes - 1)
    def _(i):
        coefficients(i, buoy[i - 1], buoy[i + 1])

    for side in range(2):
        pl.when(exists[side])(lambda side=side: rho_edge(1 - side).wait_recv())
        buoy_halo[side] = jnp.where(exists[side], 1.0 / rho_halo[side], 0.0)
    coefficients(0, buoy_halo[0], buoy[1])
    coefficients(planes - 1, buoy[planes - 2], buoy_halo[1])

    for copy in loads:
        copy.wait()

    weight = count[0].astype(jnp.float32)
    cur, old = fa, fb
    for step in range(steps):
        t = steps - 1 - step

        def advance(i, below, above, source=None, cur=cur, old=old, step=step, t=t):
            p = cur[i]
            new = coef[6, i] * p - old[i]
            if source is not None:
                new = new + source
            new = new + coef[4, i] * below + coef[5, i] * above
            new = new + coef[0, i] * pltpu.roll(p, width_x - 1, 0)
            new = new + coef[1, i] * pltpu.roll(p, 1, 0)
            new = new + coef[2, i] * pltpu.roll(p, width_y - 1, 1)
            new = new + coef[3, i] * pltpu.roll(p, 1, 1)
            old[i] = new
            term = snap[t, i].astype(jnp.float32) * new
            if step > 0:
                term = img[i] + term
            img[i] = weight * term if step == steps - 1 else term

        for side in range(2):
            pl.when(exists[side])(
                lambda side=side, step=step: edge(step, 1 - side, edge_src(now_h, side)).wait_recv()
            )
            if side == 0:
                advance(0, halo[step, 0], cur[1])
            else:
                advance(planes - 1, cur[planes - 2], halo[step, 1])
            if step < steps - 1:
                pl.when(exists[side])(
                    lambda side=side, step=step, old=old: edge(step + 1, side, edge_src(old, side)).start()
                )
        advance(1, cur[0], cur[2])
        advance(2, cur[1], cur[3], plane_src[t])

        @pl.loop(3, planes - 1)
        def _(i, advance=advance, cur=cur):
            advance(i, cur[i - 1], cur[i + 1])

        if step < steps - 1:
            for side in range(2):
                pl.when(exists[side])(
                    lambda side=side, step=step, old=old: edge(step + 1, side, edge_src(old, side)).wait_send()
                )
        cur, old = old, cur

    def to_pair(j):
        return pltpu.make_async_remote_copy(
            src_ref=slab(img, 2 * j + (1 - c)), dst_ref=pair_in.at[j],
            send_sem=pair_send.at[j], recv_sem=pair_recv.at[j],
            device_id=(d, other), device_id_type=MESH,
        )

    def to_owner(j, slot):
        return pltpu.make_async_remote_copy(
            src_ref=pair_sum.at[j], dst_ref=chain_in.at[slot],
            send_sem=chain_send.at[j], recv_sem=chain_recv.at[slot],
            device_id=(d, 2 * j + c), device_id_type=MESH,
        )

    order = [(z + j) % chain for j in range(1, chain + 1)]
    for j in order:
        to_pair(j).start()
    stores = [
        pltpu.make_async_copy(cur, out_now_h, store_sem.at[0]),
        pltpu.make_async_copy(old, out_prev_h, store_sem.at[1]),
    ]
    for copy in stores:
        copy.start()
    for n, j in enumerate(order):
        to_pair(j).wait_recv()
        at = pl.ds(pl.multiple_of((2 * j + c) * rows, 8), rows)
        pair_sum[j] = img[:, at, :] + pair_in[j]
        if n < chain - 1:
            to_owner(j, z).start()
    mine = pl.ds(pl.multiple_of(s * rows, 8), rows)
    factor = (2.0 / (4.0 * shots)) * (rho[:, mine, :] * vel[:, mine, :])
    total = pair_sum[z]
    for n in range(1, chain):
        j = (z - n + chain) % chain
        to_owner(j, j).wait_recv()
        total = total + chain_in[j]
    grad[...] = factor * total

    for copy in stores:
        copy.wait()
    for j in order:
        to_pair(j).wait_send()
    for j in order[:-1]:
        to_owner(j, z).wait_send()
    for side in range(2):

        @pl.when(exists[side])
        def _(side=side):
            edge(0, side, edge_src(now_h, side)).wait_send()
            rho_edge(side).wait_send()

    for a in range(2):
        pl.when(has_left)(lambda a=a: send(a, s, 0, True).wait_send())
        pl.when(has_right)(lambda a=a: send(a, s, 1, True).wait_send())
        send(a, s, 2, True).wait_send()
        for k in range(1, chain):

            @pl.when(z - k >= 0)
            def _(a=a, k=k):
                index = 2 * (z - k) + c
                pl.when(has_right)(lambda: send(a, index, 1).wait_send())
                send(a, index, 2).wait_send()

            @pl.when(z + k <= chain - 1)
            def _(a=a, k=k):
                index = 2 * (z + k) + c
                pl.when(has_left)(lambda: send(a, index, 0).wait_send())
                send(a, index, 2).wait_send()


def fused(adj_now, adj_prev, fwd_snap, velocity, density, shot_count, rec_x, rec_y, residual):
    depths, shots = lax.axis_size("depth"), lax.axis_size("shots")
    field = adj_now.shape[1:]
    planes, width_x, width_y = field
    steps = fwd_snap.shape[1]
    shard = velocity.shape
    chain = shots // 2
    anywhere = pl.BlockSpec(memory_space=pl.ANY)
    vmem = pl.BlockSpec(memory_space=pltpu.VMEM)
    f32 = jnp.float32
    dma = pltpu.SemaphoreType.DMA
    now, prev, grad = pl.pallas_call(
        functools.partial(kernel, depths, shots, steps),
        out_shape=(
            jax.ShapeDtypeStruct(field, f32),
            jax.ShapeDtypeStruct(field, f32),
            jax.ShapeDtypeStruct(shard, f32),
        ),
        in_specs=[anywhere] * 5 + [pl.BlockSpec(memory_space=pltpu.SMEM)] + [anywhere] * 3,
        out_specs=(anywhere, anywhere, vmem),
        scratch_shapes=[
            pltpu.VMEM(rec_x.shape, rec_x.dtype),
            pltpu.VMEM(rec_y.shape, rec_y.dtype),
            pltpu.VMEM(residual.shape[1:], f32),
            pltpu.VMEM(field, f32),
            pltpu.VMEM(field, f32),
            pltpu.VMEM((steps,) + field, fwd_snap.dtype),
            pltpu.VMEM(field, f32),
            pltpu.VMEM(field, f32),
            pltpu.VMEM(field, f32),
            pltpu.VMEM((2, width_x, width_y), f32),
            pltpu.VMEM((2, width_x, width_y), f32),
            pltpu.VMEM((steps, 2, width_x, width_y), f32),
            pltpu.VMEM((7,) + field, f32),
            pltpu.VMEM(field, f32),
            pltpu.VMEM((steps, width_x, width_y), f32),
            pltpu.VMEM((chain,) + shard, f32),
            pltpu.VMEM((chain,) + shard, f32),
            pltpu.VMEM((chain,) + shard, f32),
            dma((3,)), dma((2,)), dma((2, shots, 3)), dma((2, shots)), dma((2,)), dma((2,)),
            dma((steps, 2)), dma((steps, 2)), dma((chain,)), dma((chain,)), dma((chain,)), dma((chain,)),
            dma((2,)), dma((3,)),
        ],
        compiler_params=pltpu.CompilerParams(
            collective_id=0, has_side_effects=True, vmem_limit_bytes=60 << 20
        ),
        name="adjoint_steps",
    )(
        adj_now[0], adj_prev[0], fwd_snap[0], velocity, density, shot_count, rec_x, rec_y, residual[0]
    )
    return now[None], prev[None], grad


def chosen(*args):
    planes, rows = args[3].shape[:2]
    if rows % 8 == 0 and planes > 4 and lax.axis_size("shots") % 2 == 0:
        return fused(*args)
    return body(*args)


def solution(mesh):
    in_specs = (
        P("shots", "depth", None, None),
        P("shots", "depth", None, None),
        P("shots", None, "depth", None, None),
        P("depth", "shots", None),
        P("depth", "shots", None),
        P("shots"),
        P("shots", None),
        P("shots", None),
        P("shots", None, None),
    )
    out_specs = (
        P("shots", "depth", None, None),
        P("shots", "depth", None, None),
        P("depth", "shots", None),
    )
    return jax.shard_map(chosen, mesh=mesh, in_specs=in_specs, out_specs=out_specs, check_vma=False)
```
